32 devices in a mesh: section: 8 (over y, x, core), dp: 4 (over z).
Axes of the slice: x: 2, y: 2, z: 4, core: 2. Of those that a mesh axis runs over, the one named last changes fastest.
Arguments:
- master_weights: float32 [8, 8192, 512], P('section', 'dp'), may hold values from -0.0625 to 0.0625
- first_moment: float32 [8, 8192, 512], P('section', 'dp'), may hold values from -2 to 2
- second_moment: float32 [8, 8192, 512], P('section', 'dp'), may hold values from 0.05 to 2
- gradient_shard: float32 [8, 8192, 512], P('section', 'dp'), may hold values from -6 to 6
- hidden_states: bfloat16 [8, 2, 512, 8192], P('section', None, 'dp'), may hold values from -6 to 6
Outputs:
- new_master: float32 [8, 8192, 512], P('section', 'dp')
- new_first: float32 [8, 8192, 512], P('section', 'dp')
- new_second: float32 [8, 8192, 512], P('section', 'dp')
- hidden_out: bfloat16 [8, 2, 512, 8192], P('section', None, 'dp')
The draws below stay inside these ranges and needn't reach their ends.
All inputs are finite; a program needn't handle non-finite values.
Results may differ from the reference program's by a relative error of at most 0.008.
Values may be sent and summed in bfloat16 or wider, within the bound.
A program may use at most 192 MiB of HBM per device.

```python
import math
import jax
import jax.numpy as jnp
from jax import lax

D = 8192
KVW = 512
MB = 2
ROUNDS = 4
ADAM_STEP = 1000
SECTIONS = 8
TOKROWS = 512


def levels(own_key, shape, shards, smallest, largest):
    level, own = 1.0, jax.random.fold_in(own_key, 6)
    for axis_at, blocks in shards:
        steps = jnp.exp(jax.random.uniform(jax.random.fold_in(own, axis_at), (blocks,), jnp.float32, smallest / len(shards), largest / len(shards)))
        level = level * jnp.repeat(steps, shape[axis_at] // blocks).reshape([-1 if axis == axis_at else 1 for axis in range(len(shape))])
    return level


def normal_values(stream_key, extent, width, reach, pieces=(), held_as=jnp.bfloat16):
    gain = levels(stream_key, extent, pieces, -0.22, 0.18) if pieces else 1.0
    result = jax.random.normal(stream_key, extent, jnp.float32) * width * gain
    return jnp.minimum(jnp.maximum(result, -reach), reach).astype(held_as)


def setup_inputs(seed: int = 0) -> dict:
    keys = jax.random.split(jax.random.key(seed), 6)
    master_weights = normal_values(keys[0], (SECTIONS, D, KVW), D ** -0.5, 0.0625, ((0, 8), (1, 4)), jnp.float32)
    first_moment = normal_values(keys[1], (SECTIONS, D, KVW), 0.3, 2.0, ((0, 8), (1, 4)), jnp.float32)
    second_moment = jnp.clip(jnp.exp(math.log(2.0) - 3.6888794 * jax.random.uniform(keys[2], (SECTIONS, D, KVW), jnp.float32) ** levels(keys[2], (SECTIONS, D, KVW), ((0, 8), (1, 4)), -0.2, 0.2)), 0.05, 2.0)
    gradient_shard = normal_values(keys[3], (SECTIONS, D, KVW), 1.0, 6.0, ((0, 8), (1, 4)), jnp.float32)
    hidden_states = normal_values(keys[4], (SECTIONS, MB, TOKROWS, D), 1.0, 6.0, ((0, 8), (2, 4)))
    return {"master_weights": master_weights, "first_moment": first_moment, "second_moment": second_moment, "gradient_shard": gradient_shard, "hidden_states": hidden_states}


beta_one = 0.9
beta_two = 0.95
learn_rate = 0.0003
decay_rate = 0.1
adam_eps = 1e-08
norm_eps = 1e-05

def adamw_update(master, moment, second, gradient):
    moment_new = beta_one * moment + (1.0 - beta_one) * gradient
    second_new = beta_two * second + (1.0 - beta_two) * gradient * gradient
    corr_one = 1.0 - beta_one ** ADAM_STEP
    corr_two = 1.0 - beta_two ** ADAM_STEP
    step_size = moment_new / corr_one / (jnp.sqrt(second_new / corr_two) + adam_eps)
    master_new = master - learn_rate * (step_size + decay_rate * master)
    return (master_new, moment_new, second_new)

def layer_apply(block, weight):
    shape_in = block.shape
    flat = block.reshape(-1, shape_in[-1]).astype(jnp.float32)
    normed = (flat * lax.rsqrt(lax.optimization_barrier(jnp.mean(flat * flat, axis=-1, keepdims=True)) + norm_eps)).astype(jnp.bfloat16)
    projected = jnp.dot(normed, weight, preferred_element_type=jnp.float32).astype(jnp.bfloat16)
    update = jnp.dot(projected, weight.T, preferred_element_type=jnp.float32)
    return (flat + update).astype(jnp.bfloat16).reshape(shape_in)

def reference(master_weights, first_moment, second_moment, gradient_shard, hidden_states):
    new_master, new_first, new_second = adamw_update(master_weights, first_moment, second_moment, gradient_shard)
    weights = new_master.astype(jnp.bfloat16)
    hidden = hidden_states
    for step in range(ROUNDS):
        hidden = lax.map(lambda pair: layer_apply(pair[0], pair[1]), (hidden, weights))
        hidden = jnp.roll(hidden, 1, axis=0)
    return (new_master, new_first, new_second, hidden)
```

```python
import functools

import jax
import jax.numpy as jnp
from jax import lax
from jax.experimental import pallas as pl
from jax.experimental.pallas import tpu as pltpu
from jax.sharding import PartitionSpec as P

ROUNDS = 4
ADAM_STEP = 1000
MESH = pl.DeviceIdType.MESH


beta_one = 0.9
beta_two = 0.95
learn_rate = 0.0003
decay_rate = 0.1
adam_eps = 1e-08
norm_eps = 1e-05


def adamw_update(master, moment, second, gradient):
    moment_new = beta_one * moment + (1.0 - beta_one) * gradient
    second_new = beta_two * second + (1.0 - beta_two) * gradient * gradient
    corr_one = 1.0 - beta_one**ADAM_STEP
    corr_two = 1.0 - beta_two**ADAM_STEP
    step_size = moment_new / corr_one / (jnp.sqrt(second_new / corr_two) + adam_eps)
    master_new = master - learn_rate * (step_size + decay_rate * master)
    return (master_new, moment_new, second_new)


def relay(sections, owners, shard_ref, hidden_ref, out_ref, w, ha, hb, acc,
          load_sem, zsend, psend, precv, ysend, yrecv):
    s = lax.axis_index("section")
    r = lax.axis_index("dp")
    q = s % 4
    base = s - q
    near = q + 1 - 2 * (q % 2)
    far = (q + 2) % 4
    last = (near + 2) % 4
    near_dev = (base + near, r)
    far_dev = (base + far, r)
    ahead = ((s + 4) % sections, r)
    behind = ((s + sections - 4) % sections, r)
    rows = shard_ref.shape[0]
    width = hidden_ref.shape[2]
    count = hidden_ref.shape[0]

    def shard(slot, j):
        return w.at[slot, pl.ds(pl.multiple_of(j * rows, rows), rows)]

    def remote(slot, j, send, recv, device):
        ref = shard(slot, j)
        return pltpu.make_async_remote_copy(
            src_ref=ref, dst_ref=ref, send_sem=send, recv_sem=recv,
            device_id=device, device_id_type=MESH,
        )

    def right(j):
        return remote(q, j, zsend.at[0, j], precv.at[0, j], (s, r + 1))

    def left(j):
        return remote(q, j, zsend.at[1, j], precv.at[0, j], (s, r - 1))

    def to_far(j):
        return remote(q, j, psend.at[0, j], precv.at[1, j], far_dev)

    def to_near(j):
        return remote(q, j, psend.at[1, j], precv.at[2, j], near_dev)

    def far_to_near(j):
        return remote(far, j, psend.at[2, j], precv.at[3, j], near_dev)

    def cross(m):
        return pltpu.make_async_remote_copy(
            src_ref=ha.at[m], dst_ref=hb.at[m], send_sem=ysend.at[m],
            recv_sem=yrecv.at[m], device_id=ahead, device_id_type=MESH,
        )

    load_w = pltpu.make_async_copy(shard_ref, shard(q, r), load_sem.at[0])
    load_h = pltpu.make_async_copy(hidden_ref, ha, load_sem.at[1])
    load_w.start()
    load_h.start()

    barrier = pltpu.get_barrier_semaphore()
    partners = [near_dev, far_dev, ahead]
    if (2 * 4) % sections:
        partners.append(behind)
    for device in partners:
        pl.semaphore_signal(barrier, inc=1, device_id=device, device_id_type=MESH)

    @pl.when(r < owners - 1)
    def _():
        pl.semaphore_signal(barrier, inc=1, device_id=(s, r + 1), device_id_type=MESH)

    @pl.when(r > 0)
    def _():
        pl.semaphore_signal(barrier, inc=1, device_id=(s, r - 1), device_id_type=MESH)

    along = jnp.minimum(r, 1) + jnp.minimum(owners - 1 - r, 1)
    pl.semaphore_wait(barrier, len(partners) + along)

    load_w.wait()
    for k in range(owners):
        low, high = r - k, r + k

        @pl.when(low >= 0)
        def _(low=low, k=k):
            if k:
                left(low).wait_recv()

            @pl.when(r < owners - 1)
            def _():
                right(low).start()

        @pl.when(high < owners)
        def _(high=high, k=k):
            if k:
                left(high).wait_recv()

            @pl.when(r > 0)
            def _():
                left(high).start()

        @pl.when(low >= 0)
        def _(low=low):
            to_far(low).start()
            to_near(low).start()

        if k:
            @pl.when(high < owners)
            def _(high=high):
                to_far(high).start()
                to_near(high).start()

    @pl.loop(0, owners)
    def _(j):
        to_near(j).wait_recv()

    load_h.wait()

    deep = 2048
    wide = 1024

    def apply(buf, m, t):
        acc[...] = jnp.zeros_like(acc)

        def project(i, total):
            at = pl.ds(pl.multiple_of(i * deep, deep), deep)
            x = buf[m, :, at]
            acc[...] += jnp.dot(x, w[t, at, :], preferred_element_type=jnp.float32)
            flat = x.astype(jnp.float32)
            return total + jnp.sum(flat * flat, axis=-1, keepdims=True)

        total = lax.fori_loop(
            0, width // deep, project, jnp.zeros((buf.shape[1], 1), jnp.float32)
        )
        scale = lax.rsqrt(total * (1.0 / width) + norm_eps)
        projected = (acc[...] * scale).astype(jnp.bfloat16)

        @pl.loop(0, width // wide)
        def _(i):
            at = pl.ds(pl.multiple_of(i * wide, wide), wide)
            update = lax.dot_general(
                projected, w[t, at, :], (((1,), (1,)), ((), ())),
                preferred_element_type=jnp.float32,
            )
            buf[m, :, at] = (buf[m, :, at].astype(jnp.float32) + update).astype(jnp.bfloat16)

    pair = q // 2

    @pl.loop(0, count)
    def _(m):
        @pl.loop(q, pair * 2 + 2)
        def _(t):
            apply(ha, m, t)

        @pl.when(pair == 1)
        def _():
            cross(m).start()

    for k in range(owners):
        low, high = r - k, r + k

        @pl.when(low >= 0)
        def _(low=low):
            to_far(low).wait_recv()
            far_to_near(low).start()

        if k:
            @pl.when(high < owners)
            def _(high=high):
                to_far(high).wait_recv()
                far_to_near(high).start()

    @pl.loop(0, owners)
    def _(j):
        far_to_near(j).wait_recv()

    @pl.when(pair == 0)
    def _():
        @pl.loop(0, count)
        def _(m):
            @pl.loop(2, 4)
            def _(t):
                apply(ha, m, t)

            cross(m).start()

    @pl.loop(0, count)
    def _(m):
        cross(m).wait_recv()

        @pl.loop(0, q)
        def _(t):
            apply(hb, m, t)

        pltpu.make_async_copy(hb.at[m], out_ref.at[m], load_sem.at[2 + m]).start()

    @pl.loop(0, count)
    def _(m):
        cross(m).wait_send()
        pltpu.make_async_copy(hb.at[m], out_ref.at[m], load_sem.at[2 + m]).wait()

    @pl.loop(0, owners)
    def _(j):
        to_far(j).wait_send()
        to_near(j).wait_send()
        far_to_near(j).wait_send()

        @pl.when((j <= r) & (r < owners - 1))
        def _():
            right(j).wait_send()

        @pl.when((j >= r) & (r > 0))
        def _():
            left(j).wait_send()


def per_device(sections, owners, master_weights, first_moment, second_moment, gradient_shard,
               hidden_states):
    new_master, new_first, new_second = adamw_update(
        master_weights, first_moment, second_moment, gradient_shard
    )
    local_rows = new_master[0].astype(jnp.bfloat16)
    hidden = hidden_states[0]
    count, block, width = hidden.shape
    columns = local_rows.shape[1]
    moved = pl.pallas_call(
        functools.partial(relay, sections, owners),
        out_shape=jax.ShapeDtypeStruct(hidden.shape, hidden.dtype),
        in_specs=[pl.BlockSpec(memory_space=pl.ANY)] * 2,
        out_specs=pl.BlockSpec(memory_space=pl.ANY),
        scratch_shapes=[
            pltpu.VMEM((4, width, columns), jnp.bfloat16),
            pltpu.VMEM((count, block, width), jnp.bfloat16),
            pltpu.VMEM((count, block, width), jnp.bfloat16),
            pltpu.VMEM((block, columns), jnp.float32),
            pltpu.SemaphoreType.DMA((2 + count,)),
            pltpu.SemaphoreType.DMA((2, owners)),
            pltpu.SemaphoreType.DMA((3, owners)),
            pltpu.SemaphoreType.DMA((4, owners)),
            pltpu.SemaphoreType.DMA((count,)),
            pltpu.SemaphoreType.DMA((count,)),
        ],
        compiler_params=pltpu.CompilerParams(
            collective_id=0, has_side_effects=True, vmem_limit_bytes=56 * 1024 * 1024
        ),
        cost_estimate=pl.CostEstimate(
            flops=ROUNDS * count * block * width * columns * 4,
            bytes_accessed=4 * count * block * width,
            transcendentals=0,
        ),
    )(local_rows, hidden)
    return (new_master, new_first, new_second, moved[None])


def solution(mesh):
    placed = (
        P("section", "dp", None),
        P("section", "dp", None),
        P("section", "dp", None),
        P("section", "dp", None),
        P("section", None, "dp", None),
    )
    return jax.shard_map(
        functools.partial(per_device, mesh.shape["section"], mesh.shape["dp"]),
        mesh=mesh,
        in_specs=placed,
        out_specs=(
            P("section", "dp", None),
            P("section", "dp", None),
            P("section", "dp", None),
            P("section", None, "dp", None),
        ),
        check_vma=False,
    )
```

```python
import functools

import jax
import jax.numpy as jnp
from jax import lax
from jax.experimental import pallas as pl
from jax.experimental.pallas import tpu as pltpu
from jax.sharding import PartitionSpec as P

ROUNDS = 4
ADAM_STEP = 1000
MESH = pl.DeviceIdType.MESH


beta_one = 0.9
beta_two = 0.95
learn_rate = 0.0003
decay_rate = 0.1
adam_eps = 1e-08
norm_eps = 1e-05


def adamw_update(master, moment, second, gradient):
    moment_new = beta_one * moment + (1.0 - beta_one) * gradient
    second_new = beta_two * second + (1.0 - beta_two) * gradient * gradient
    corr_one = 1.0 - beta_one**ADAM_STEP
    corr_two = 1.0 - beta_two**ADAM_STEP
    step_size = moment_new / corr_one / (jnp.sqrt(second_new / corr_two) + adam_eps)
    master_new = master - learn_rate * (step_size + decay_rate * master)
    return (master_new, moment_new, second_new)


def relay(sections, owners, shard_ref, hidden_ref, out_ref, w, ha, hb, acc,
          load_sem, zsend, psend, precv, ysend, yrecv, osem):
    s = lax.axis_index("section")
    r = lax.axis_index("dp")
    q = s % 4
    base = s - q
    near = q + 1 - 2 * (q % 2)
    far = (q + 2) % 4
    last = (near + 2) % 4
    near_dev = (base + near, r)
    far_dev = (base + far, r)
    ahead = ((s + 4) % sections, r)
    behind = ((s + sections - 4) % sections, r)
    rows = shard_ref.shape[0]
    width = hidden_ref.shape[2]
    count, block = hidden_ref.shape[0], hidden_ref.shape[1]
    chunks = ysend.shape[1]
    chunk = width // chunks

    def shard(slot, j):
        return w.at[slot, pl.ds(pl.multiple_of(j * rows, rows), rows)]

    def remote(slot, j, send, recv, device):
        ref = shard(slot, j)
        return pltpu.make_async_remote_copy(
            src_ref=ref, dst_ref=ref, send_sem=send, recv_sem=recv,
            device_id=device, device_id_type=MESH,
        )

    def right(j):
        return remote(q, j, zsend.at[0, j], precv.at[0, j], (s, r + 1))

    def left(j):
        return remote(q, j, zsend.at[1, j], precv.at[0, j], (s, r - 1))

    half = rows // 2

    def part(slot, j, lower, send, recv, device):
        ref = w.at[slot, pl.ds(pl.multiple_of(j * rows + lower * half, half), half)]
        return pltpu.make_async_remote_copy(
            src_ref=ref, dst_ref=ref, send_sem=send, recv_sem=recv,
            device_id=device, device_id_type=MESH,
        )

    def to_far(j, k):
        if k == 1:
            return part(q, j, 0, psend.at[0, j], precv.at[1, j], far_dev)
        return remote(q, j, psend.at[0, j], precv.at[1, j], far_dev)

    def lower_right(j):
        return part(far, j, 1, zsend.at[2, j], precv.at[4, j], (s, r + 1))

    def lower_left(j):
        return part(far, j, 1, zsend.at[3, j], precv.at[4, j], (s, r - 1))

    def at_distance(k, use):
        @pl.when(r - k >= 0)
        def _():
            use(r - k)

        if k:
            @pl.when(r + k < owners)
            def _():
                use(r + k)

    def to_near(j):
        return remote(q, j, psend.at[1, j], precv.at[2, j], near_dev)

    def far_to_near(j):
        return remote(far, j, psend.at[2, j], precv.at[3, j], near_dev)

    def columns(c):
        return pl.ds(pl.multiple_of(c * chunk, chunk), chunk)

    def cross(m, c):
        return pltpu.make_async_remote_copy(
            src_ref=ha.at[m, :, columns(c)], dst_ref=hb.at[m, :, columns(c)],
            send_sem=ysend.at[m, c], recv_sem=yrecv.at[m, c],
            device_id=ahead, device_id_type=MESH,
        )

    def store(m, c):
        return pltpu.make_async_copy(
            hb.at[m, :, columns(c)], out_ref.at[m, :, columns(c)], osem.at[m, c]
        )

    load_w = pltpu.make_async_copy(shard_ref, shard(q, r), load_sem.at[0])
    load_h = pltpu.make_async_copy(hidden_ref, ha, load_sem.at[1])
    load_w.start()
    load_h.start()

    barrier = pltpu.get_barrier_semaphore()
    partners = [near_dev, far_dev, ahead]
    if (2 * 4) % sections:
        partners.append(behind)
    for device in partners:
        pl.semaphore_signal(barrier, inc=1, device_id=device, device_id_type=MESH)

    @pl.when(r < owners - 1)
    def _():
        pl.semaphore_signal(barrier, inc=1, device_id=(s, r + 1), device_id_type=MESH)

    @pl.when(r > 0)
    def _():
        pl.semaphore_signal(barrier, inc=1, device_id=(s, r - 1), device_id_type=MESH)

    along = jnp.minimum(r, 1) + jnp.minimum(owners - 1 - r, 1)
    pl.semaphore_wait(barrier, len(partners) + along)

    load_w.wait()
    for k in range(owners):
        low, high = r - k, r + k

        @pl.when(low >= 0)
        def _(low=low, k=k):
            if k:
                left(low).wait_recv()

            @pl.when(r < owners - 1)
            def _():
                right(low).start()

        @pl.when(high < owners)
        def _(high=high, k=k):
            if k:
                left(high).wait_recv()

            @pl.when(r > 0)
            def _():
                left(high).start()

        def send_on(j, k=k):
            to_far(j, k).start()
            to_near(j).start()

        at_distance(k, send_on)

    to_far(r, 0).wait_recv()
    far_to_near(r).start()

    @pl.when(r > 0)
    def _():
        left(owners - 1).wait_send()
        lower_left(r).start()

    @pl.when(r < owners - 1)
    def _():
        right(0).wait_send()
        lower_right(r).start()

    def hand_on(k):
        def use(j):
            to_far(j, k).wait_recv()
            if k == 1:
                lower_left(j).wait_recv()
            far_to_near(j).start()

        at_distance(k, use)

    for k in range(2, owners - 1):
        hand_on(k)

    @pl.loop(0, owners)
    def _(j):
        to_near(j).wait_recv()

    load_h.wait()

    def apply(buf, t, first, many, before, after):
        tall = many * block
        here = pl.ds(first, many)
        acc[:tall] = jnp.zeros((tall, acc.shape[1]), jnp.float32)

        def project(c, total):
            before(c)
            x = buf[here, :, columns(c)].reshape(tall, chunk)
            acc[:tall] += jnp.dot(x, w[t, columns(c), :], preferred_element_type=jnp.float32)
            flat = x.astype(jnp.float32)
            return total + jnp.sum(flat * flat, axis=-1, keepdims=True)

        total = lax.fori_loop(0, chunks, project, jnp.zeros((tall, 1), jnp.float32))
        scale = lax.rsqrt(total * (1.0 / width) + norm_eps)
        projected = (acc[:tall] * scale).astype(jnp.bfloat16)

        @pl.loop(0, chunks)
        def _(c):
            update = lax.dot_general(
                projected, w[t, columns(c), :], (((1,), (1,)), ((), ())),
                preferred_element_type=jnp.float32,
            )
            x = buf[here, :, columns(c)].reshape(tall, chunk).astype(jnp.float32)
            buf[here, :, columns(c)] = (x + update).astype(jnp.bfloat16).reshape(many, block, chunk)
            after(c)

    def nothing(c):
        pass

    pair = q // 2

    @pl.loop(q, pair * 2 + 2)
    def _(t):
        def after(c):
            @pl.when(t == 3)
            def _():
                for m in range(count):
                    cross(m, c).start()

        apply(ha, t, 0, count, nothing, after)

    for k in range(1, owners):
        if k == 1 or k == owners - 1:
            hand_on(k)

    @pl.loop(0, owners)
    def _(j):
        far_to_near(j).wait_recv()

    @pl.when(pair == 0)
    def _():
        @pl.loop(0, count)
        def _(m):
            @pl.loop(2, 4)
            def _(t):
                def after(c):
                    @pl.when(t == 3)
                    def _():
                        cross(m, c).start()

                apply(ha, t, m, 1, nothing, after)

    @pl.loop(0, count)
    def _(m):
        @pl.loop(0, q)
        def _(t):
            def before(c):
                @pl.when(t == 0)
                def _():
                    cross(m, c).wait_recv()

            def after(c):
                @pl.when(t == q - 1)
                def _():
                    store(m, c).start()

            apply(hb, t, m, 1, before, after)

        @pl.when(q == 0)
        def _():
            @pl.loop(0, chunks)
            def _(c):
                cross(m, c).wait_recv()
                store(m, c).start()

    @pl.loop(0, count)
    def _(m):
        @pl.loop(0, chunks)
        def _(c):
            cross(m, c).wait_send()
            store(m, c).wait()

    for k in range(owners):
        def drain(j, k=k):
            to_far(j, k).wait_send()
            to_near(j).wait_send()
            far_to_near(j).wait_send()

        at_distance(k, drain)

    @pl.loop(0, owners)
    def _(j):
        @pl.when((j > 0) & (j <= r) & (r < owners - 1))
        def _():
            right(j).wait_send()

        @pl.when((j < owners - 1) & (j >= r) & (r > 0))
        def _():
            left(j).wait_send()

    @pl.when(r > 0)
    def _():
        lower_left(r).wait_send()

    @pl.when(r < owners - 1)
    def _():
        lower_right(r).wait_send()


def per_device(sections, owners, master_weights, first_moment, second_moment, gradient_shard,
               hidden_states):
    new_master, new_first, new_second = adamw_update(
        master_weights, first_moment, second_moment, gradient_shard
    )
    local_rows = new_master[0].astype(jnp.bfloat16)
    hidden = hidden_states[0]
    count, block, width = hidden.shape
    columns = local_rows.shape[1]
    chunks = width // 1024
    moved = pl.pallas_call(
        functools.partial(relay, sections, owners),
        out_shape=jax.ShapeDtypeStruct(hidden.shape, hidden.dtype),
        in_specs=[pl.BlockSpec(memory_space=pl.ANY)] * 2,
        out_specs=pl.BlockSpec(memory_space=pl.ANY),
        scratch_shapes=[
            pltpu.VMEM((4, width, columns), jnp.bfloat16),
            pltpu.VMEM((count, block, width), jnp.bfloat16),
            pltpu.VMEM((count, block, width), jnp.bfloat16),
            pltpu.VMEM((count * block, columns), jnp.float32),
            pltpu.SemaphoreType.DMA((2,)),
            pltpu.SemaphoreType.DMA((4, owners)),
            pltpu.SemaphoreType.DMA((3, owners)),
            pltpu.SemaphoreType.DMA((5, owners)),
            pltpu.SemaphoreType.DMA((count, chunks)),
            pltpu.SemaphoreType.DMA((count, chunks)),
            pltpu.SemaphoreType.DMA((count, chunks)),
        ],
        compiler_params=pltpu.CompilerParams(
            collective_id=0, has_side_effects=True, vmem_limit_bytes=56 * 1024 * 1024
        ),
        cost_estimate=pl.CostEstimate(
            flops=ROUNDS * count * block * width * columns * 4,
            bytes_accessed=4 * count * block * width,
            transcendentals=0,
        ),
    )(local_rows, hidden)
    return (new_master, new_first, new_second, moved[None])


def solution(mesh):
    placed = (
        P("section", "dp", None),
        P("section", "dp", None),
        P("section", "dp", None),
        P("section", "dp", None),
        P("section", None, "dp", None),
    )
    return jax.shard_map(
        functools.partial(per_device, mesh.shape["section"], mesh.shape["dp"]),
        mesh=mesh,
        in_specs=placed,
        out_specs=(
            P("section", "dp", None),
            P("section", "dp", None),
            P("section", "dp", None),
            P("section", None, "dp", None),
        ),
        check_vma=False,
    )
```

```python
import functools

import jax
import jax.numpy as jnp
from jax import lax
from jax.experimental import pallas as pl
from jax.experimental.pallas import tpu as pltpu
from jax.sharding import PartitionSpec as P

ROUNDS = 4
ADAM_STEP = 1000
MESH = pl.DeviceIdType.MESH


beta_one = 0.9
beta_two = 0.95
learn_rate = 0.0003
decay_rate = 0.1
adam_eps = 1e-08
norm_eps = 1e-05


def adamw_update(master, moment, second, gradient):
    moment_new = beta_one * moment + (1.0 - beta_one) * gradient
    second_new = beta_two * second + (1.0 - beta_two) * gradient * gradient
    corr_one = 1.0 - beta_one**ADAM_STEP
    corr_two = 1.0 - beta_two**ADAM_STEP
    step_size = moment_new / corr_one / (jnp.sqrt(second_new / corr_two) + adam_eps)
    master_new = master - learn_rate * (step_size + decay_rate * master)
    return (master_new, moment_new, second_new)


def relay(sections, owners, shard_ref, hidden_ref, out_ref, w, ha, hb, acc,
          load_sem, zsend, psend, precv, ysend, yrecv, osem):
    s = lax.axis_index("section")
    r = lax.axis_index("dp")
    q = s % 4
    base = s - q
    near = q + 1 - 2 * (q % 2)
    far = (q + 2) % 4
    last = (near + 2) % 4
    near_dev = (base + near, r)
    far_dev = (base + far, r)
    ahead = ((s + 4) % sections, r)
    behind = ((s + sections - 4) % sections, r)
    rows = shard_ref.shape[0]
    width = hidden_ref.shape[2]
    count, block = hidden_ref.shape[0], hidden_ref.shape[1]
    chunks = ysend.shape[1]
    chunk = width // chunks

    half = rows // 2

    def piece(slot, g, send, recv, device):
        ref = w.at[slot, pl.ds(pl.multiple_of(g * half, half), half)]
        return pltpu.make_async_remote_copy(
            src_ref=ref, dst_ref=ref, send_sem=send, recv_sem=recv,
            device_id=device, device_id_type=MESH,
        )

    def right(g):
        return piece(q, g, zsend.at[0, g], precv.at[0, g], (s, r + 1))

    def left(g):
        return piece(q, g, zsend.at[1, g], precv.at[0, g], (s, r - 1))

    def to_far(g):
        return piece(q, g, psend.at[0, g], precv.at[1, g], far_dev)

    def to_near(g):
        return piece(q, g, psend.at[1, g], precv.at[2, g], near_dev)

    def far_to_near(g):
        return piece(far, g, psend.at[2, g], precv.at[3, g], near_dev)

    def lower_right(g):
        return piece(far, g, zsend.at[2, g], precv.at[4, g], (s, r + 1))

    def lower_left(g):
        return piece(far, g, zsend.at[3, g], precv.at[4, g], (s, r - 1))

    def at_distance(k, use):
        @pl.when(r - k >= 0)
        def _():
            use(r - k)

        if k:
            @pl.when(r + k < owners)
            def _():
                use(r + k)

    def columns(c):
        return pl.ds(pl.multiple_of(c * chunk, chunk), chunk)

    def cross(m, c):
        return pltpu.make_async_remote_copy(
            src_ref=ha.at[m, :, columns(c)], dst_ref=hb.at[m, :, columns(c)],
            send_sem=ysend.at[m, c], recv_sem=yrecv.at[m, c],
            device_id=ahead, device_id_type=MESH,
        )

    def store(m, c):
        return pltpu.make_async_copy(
            hb.at[m, :, columns(c)], out_ref.at[m, :, columns(c)], osem.at[m, c]
        )

    own = w.at[q, pl.ds(pl.multiple_of(r * rows, rows), rows)]
    load_w = pltpu.make_async_copy(shard_ref, own, load_sem.at[0])
    load_h = pltpu.make_async_copy(hidden_ref, ha, load_sem.at[1])
    load_w.start()
    load_h.start()

    barrier = pltpu.get_barrier_semaphore()
    partners = [near_dev, far_dev, ahead]
    if (2 * 4) % sections:
        partners.append(behind)
    for device in partners:
        pl.semaphore_signal(barrier, inc=1, device_id=device, device_id_type=MESH)

    @pl.when(r < owners - 1)
    def _():
        pl.semaphore_signal(barrier, inc=1, device_id=(s, r + 1), device_id_type=MESH)

    @pl.when(r > 0)
    def _():
        pl.semaphore_signal(barrier, inc=1, device_id=(s, r - 1), device_id_type=MESH)

    along = jnp.minimum(r, 1) + jnp.minimum(owners - 1 - r, 1)
    pl.semaphore_wait(barrier, len(partners) + along)

    load_w.wait()
    for i in range(2 * owners):
        k, h = divmod(i, 2)
        before_k, before_h = divmod(i - 1, 2)

        def arrive(j, i=i, h=h):
            g = 2 * j + h
            if i >= 2:
                left(g).wait_recv()
            if i != 3:
                to_far(g).start()
            to_near(g).start()

        at_distance(k, arrive)

        @pl.when((r > 0) & (r + k < owners))
        def _(i=i, k=k, h=h, before_k=before_k, before_h=before_h):
            if i:
                left(2 * (r + before_k) + before_h).wait_send()
            left(2 * (r + k) + h).start()

        @pl.when((r < owners - 1) & (r - k >= 0))
        def _(i=i, k=k, h=h, before_k=before_k, before_h=before_h):
            if i:
                right(2 * (r - before_k) + before_h).wait_send()
            right(2 * (r - k) + h).start()

        if i == 2:
            for g in (2 * r, 2 * r + 1):
                to_far(g).wait_recv()
                far_to_near(g).start()

        if i >= 2 and h == 0:
            @pl.when((r > 0) & (r + k == owners))
            def _():
                left(2 * owners - 1).wait_send()
                lower_left(2 * r + 1).start()

            @pl.when((r < owners - 1) & (r - k == -1))
            def _():
                right(1).wait_send()
                lower_right(2 * r + 1).start()

    def hand_on(k, h):
        def use(j):
            g = 2 * j + h
            if (k, h) == (1, 1):
                lower_left(g).wait_recv()
            else:
                to_far(g).wait_recv()
            far_to_near(g).start()

        at_distance(k, use)

    hand_on(1, 0)
    for k in range(2, owners - 1):
        hand_on(k, 0)
        hand_on(k, 1)

    @pl.loop(0, 2 * owners)
    def _(j):
        to_near(j).wait_recv()

    load_h.wait()

    def apply(buf, t, first, many, before, after):
        tall = many * block
        here = pl.ds(first, many)
        acc[:tall] = jnp.zeros((tall, acc.shape[1]), jnp.float32)

        def project(c, total):
            before(c)
            x = buf[here, :, columns(c)].reshape(tall, chunk)
            acc[:tall] += jnp.dot(x, w[t, columns(c), :], preferred_element_type=jnp.float32)
            flat = x.astype(jnp.float32)
            return total + jnp.sum(flat * flat, axis=-1, keepdims=True)

        total = lax.fori_loop(0, chunks, project, jnp.zeros((tall, 1), jnp.float32))
        scale = lax.rsqrt(total * (1.0 / width) + norm_eps)
        projected = (acc[:tall] * scale).astype(jnp.bfloat16)

        @pl.loop(0, chunks)
        def _(c):
            update = lax.dot_general(
                projected, w[t, columns(c), :], (((1,), (1,)), ((), ())),
                preferred_element_type=jnp.float32,
            )
            x = buf[here, :, columns(c)].reshape(tall, chunk).astype(jnp.float32)
            buf[here, :, columns(c)] = (x + update).astype(jnp.bfloat16).reshape(many, block, chunk)
            after(c)

    def nothing(c):
        pass

    pair = q // 2

    @pl.when(pair == 0)
    def _():
        @pl.loop(q, 2)
        def _(t):
            apply(ha, t, 0, count, nothing, nothing)

    @pl.when(pair == 1)
    def _():
        @pl.loop(0, count)
        def _(m):
            @pl.loop(q, 4)
            def _(t):
                def after(c):
                    @pl.when(t == 3)
                    def _():
                        cross(m, c).start()

                apply(ha, t, m, 1, nothing, after)

    if owners > 2:
        hand_on(owners - 1, 0)
    hand_on(1, 1)
    if owners > 2:
        hand_on(owners - 1, 1)

    @pl.loop(0, 2 * owners)
    def _(j):
        far_to_near(j).wait_recv()

    @pl.when(pair == 0)
    def _():
        @pl.loop(0, count)
        def _(m):
            @pl.loop(2, 4)
            def _(t):
                def after(c):
                    @pl.when(t == 3)
                    def _():
                        cross(m, c).start()

                apply(ha, t, m, 1, nothing, after)

    @pl.loop(0, count)
    def _(m):
        @pl.loop(0, q)
        def _(t):
            def before(c):
                @pl.when(t == 0)
                def _():
                    cross(m, c).wait_recv()

            def after(c):
                @pl.when(t == q - 1)
                def _():
                    store(m, c).start()

            apply(hb, t, m, 1, before, after)

        @pl.when(q == 0)
        def _():
            @pl.loop(0, chunks)
            def _(c):
                cross(m, c).wait_recv()
                store(m, c).start()

    @pl.loop(0, count)
    def _(m):
        @pl.loop(0, chunks)
        def _(c):
            cross(m, c).wait_send()
            store(m, c).wait()

    for i in range(2 * owners):
        def drain(j, i=i):
            g = 2 * j + i % 2
            if i != 3:
                to_far(g).wait_send()
            to_near(g).wait_send()
            far_to_near(g).wait_send()

        at_distance(i // 2, drain)

    @pl.when(r > 0)
    def _():
        lower_left(2 * r + 1).wait_send()

    @pl.when(r < owners - 1)
    def _():
        lower_right(2 * r + 1).wait_send()


def per_device(sections, owners, master_weights, first_moment, second_moment, gradient_shard,
               hidden_states):
    new_master, new_first, new_second = adamw_update(
        master_weights, first_moment, second_moment, gradient_shard
    )
    local_rows = new_master[0].astype(jnp.bfloat16)
    hidden = hidden_states[0]
    count, block, width = hidden.shape
    columns = local_rows.shape[1]
    chunks = width // 1024
    moved = pl.pallas_call(
        functools.partial(relay, sections, owners),
        out_shape=jax.ShapeDtypeStruct(hidden.shape, hidden.dtype),
        in_specs=[pl.BlockSpec(memory_space=pl.ANY)] * 2,
        out_specs=pl.BlockSpec(memory_space=pl.ANY),
        scratch_shapes=[
            pltpu.VMEM((4, width, columns), jnp.bfloat16),
            pltpu.VMEM((count, block, width), jnp.bfloat16),
            pltpu.VMEM((count, block, width), jnp.bfloat16),
            pltpu.VMEM((count * block, columns), jnp.float32),
            pltpu.SemaphoreType.DMA((2,)),
            pltpu.SemaphoreType.DMA((4, 2 * owners)),
            pltpu.SemaphoreType.DMA((3, 2 * owners)),
            pltpu.SemaphoreType.DMA((5, 2 * owners)),
            pltpu.SemaphoreType.DMA((count, chunks)),
            pltpu.SemaphoreType.DMA((count, chunks)),
            pltpu.SemaphoreType.DMA((count, chunks)),
        ],
        compiler_params=pltpu.CompilerParams(
            collective_id=0, has_side_effects=True, vmem_limit_bytes=56 * 1024 * 1024
        ),
        cost_estimate=pl.CostEstimate(
            flops=ROUNDS * count * block * width * columns * 4,
            bytes_accessed=4 * count * block * width,
            transcendentals=0,
        ),
    )(local_rows, hidden)
    return (new_master, new_first, new_second, moved[None])


def solution(mesh):
    placed = (
        P("section", "dp", None),
        P("section", "dp", None),
        P("section", "dp", None),
        P("section", "dp", None),
        P("section", None, "dp", None),
    )
    return jax.shard_map(
        functools.partial(per_device, mesh.shape["section"], mesh.shape["dp"]),
        mesh=mesh,
        in_specs=placed,
        out_specs=(
            P("section", "dp", None),
            P("section", "dp", None),
            P("section", "dp", None),
            P("section", None, "dp", None),
        ),
        check_vma=False,
    )
```

```python
import functools

import jax
import jax.numpy as jnp
from jax import lax
from jax.experimental import pallas as pl
from jax.experimental.pallas import tpu as pltpu
from jax.sharding import PartitionSpec as P

ROUNDS = 4
ADAM_STEP = 1000
MESH = pl.DeviceIdType.MESH


beta_one = 0.9
beta_two = 0.95
learn_rate = 0.0003
decay_rate = 0.1
adam_eps = 1e-08
norm_eps = 1e-05


def adamw_update(master, moment, second, gradient):
    moment_new = beta_one * moment + (1.0 - beta_one) * gradient
    second_new = beta_two * second + (1.0 - beta_two) * gradient * gradient
    corr_one = 1.0 - beta_one**ADAM_STEP
    corr_two = 1.0 - beta_two**ADAM_STEP
    step_size = moment_new / corr_one / (jnp.sqrt(second_new / corr_two) + adam_eps)
    master_new = master - learn_rate * (step_size + decay_rate * master)
    return (master_new, moment_new, second_new)


def relay(sections, owners, shard_ref, hidden_ref, out_ref, w, ha, hb, acc,
          load_sem, zsend, psend, precv, ysend, yrecv, osem):
    s = lax.axis_index("section")
    r = lax.axis_index("dp")
    q = s % 4
    base = s - q
    near = q + 1 - 2 * (q % 2)
    far = (q + 2) % 4
    last = (near + 2) % 4
    near_dev = (base + near, r)
    far_dev = (base + far, r)
    ahead = ((s + 4) % sections, r)
    behind = ((s + sections - 4) % sections, r)
    rows = shard_ref.shape[0]
    width = hidden_ref.shape[2]
    count, block = hidden_ref.shape[0], hidden_ref.shape[1]
    chunks = ysend.shape[1]
    chunk = width // chunks

    half = rows // 2

    def piece(slot, g, send, recv, device):
        ref = w.at[slot, pl.ds(pl.multiple_of(g * half, half), half)]
        return pltpu.make_async_remote_copy(
            src_ref=ref, dst_ref=ref, send_sem=send, recv_sem=recv,
            device_id=device, device_id_type=MESH,
        )

    def right(g):
        return piece(q, g, zsend.at[0, g], precv.at[0, g], (s, r + 1))

    def left(g):
        return piece(q, g, zsend.at[1, g], precv.at[0, g], (s, r - 1))

    def to_far(g):
        return piece(q, g, psend.at[0, g], precv.at[1, g], far_dev)

    def to_near(g):
        return piece(q, g, psend.at[1, g], precv.at[2, g], near_dev)

    def far_to_near(g):
        return piece(far, g, psend.at[2, g], precv.at[3, g], near_dev)

    def lower_right(g):
        return piece(far, g, zsend.at[2, g], precv.at[4, g], (s, r + 1))

    def lower_left(g):
        return piece(far, g, zsend.at[3, g], precv.at[4, g], (s, r - 1))

    def at_distance(k, use):
        @pl.when(r - k >= 0)
        def _():
            use(r - k)

        if k:
            @pl.when(r + k < owners)
            def _():
                use(r + k)

    def columns(c):
        return pl.ds(pl.multiple_of(c * chunk, chunk), chunk)

    def cross(m, c):
        return pltpu.make_async_remote_copy(
            src_ref=ha.at[m, :, columns(c)], dst_ref=hb.at[m, :, columns(c)],
            send_sem=ysend.at[m, c], recv_sem=yrecv.at[m, c],
            device_id=ahead, device_id_type=MESH,
        )

    def store(m, c):
        return pltpu.make_async_copy(
            hb.at[m, :, columns(c)], out_ref.at[m, :, columns(c)], osem.at[m, c]
        )

    own = w.at[q, pl.ds(pl.multiple_of(r * rows, rows), rows)]
    load_w = pltpu.make_async_copy(shard_ref, own, load_sem.at[0])
    load_h = pltpu.make_async_copy(hidden_ref, ha, load_sem.at[1])
    load_w.start()
    load_h.start()

    barrier = pltpu.get_barrier_semaphore()
    partners = [near_dev, far_dev, ahead]
    if (2 * 4) % sections:
        partners.append(behind)
    for device in partners:
        pl.semaphore_signal(barrier, inc=1, device_id=device, device_id_type=MESH)

    @pl.when(r < owners - 1)
    def _():
        pl.semaphore_signal(barrier, inc=1, device_id=(s, r + 1), device_id_type=MESH)

    @pl.when(r > 0)
    def _():
        pl.semaphore_signal(barrier, inc=1, device_id=(s, r - 1), device_id_type=MESH)

    along = jnp.minimum(r, 1) + jnp.minimum(owners - 1 - r, 1)
    pl.semaphore_wait(barrier, len(partners) + along)

    load_w.wait()
    for i in range(2 * owners):
        k, h = divmod(i, 2)
        before_k, before_h = divmod(i - 1, 2)

        def arrive(j, i=i, h=h):
            g = 2 * j + h
            if i >= 2:
                left(g).wait_recv()
            if i != 3:
                to_far(g).start()
            to_near(g).start()

        at_distance(k, arrive)

        @pl.when((r > 0) & (r + k < owners))
        def _(i=i, k=k, h=h, before_k=before_k, before_h=before_h):
            if i:
                left(2 * (r + before_k) + before_h).wait_send()
            left(2 * (r + k) + h).start()

        @pl.when((r < owners - 1) & (r - k >= 0))
        def _(i=i, k=k, h=h, before_k=before_k, before_h=before_h):
            if i:
                right(2 * (r - before_k) + before_h).wait_send()
            right(2 * (r - k) + h).start()

        if i == 2:
            for g in (2 * r, 2 * r + 1):
                to_far(g).wait_recv()
                far_to_near(g).start()

        if i >= 2 and h == 0:
            @pl.when((r > 0) & (r + k == owners))
            def _():
                left(2 * owners - 1).wait_send()
                lower_left(2 * r + 1).start()

            @pl.when((r < owners - 1) & (r - k == -1))
            def _():
                right(1).wait_send()
                lower_right(2 * r + 1).start()

    def hand_on(k, h):
        def use(j):
            g = 2 * j + h
            if (k, h) == (1, 1):
                lower_left(g).wait_recv()
            else:
                to_far(g).wait_recv()
            far_to_near(g).start()

        at_distance(k, use)

    hand_on(1, 0)
    for k in range(2, owners - 1):
        hand_on(k, 0)
        hand_on(k, 1)

    @pl.loop(0, 2 * owners)
    def _(j):
        to_near(j).wait_recv()

    load_h.wait()

    def apply(buf, t, first, many, before, after):
        tall = many * block
        here = pl.ds(first, many)
        acc[:tall] = jnp.zeros((tall, acc.shape[1]), jnp.float32)

        def project(c, total):
            before(c)
            x = buf[here, :, columns(c)].reshape(tall, chunk)
            acc[:tall] += jnp.dot(x, w[t, columns(c), :], preferred_element_type=jnp.float32)
            flat = x.astype(jnp.float32)
            return total + jnp.sum(flat * flat, axis=-1, keepdims=True)

        total = lax.fori_loop(0, chunks, project, jnp.zeros((tall, 1), jnp.float32))
        scale = lax.rsqrt(total * (1.0 / width) + norm_eps)
        projected = (acc[:tall] * scale).astype(jnp.bfloat16)

        @pl.loop(0, chunks)
        def _(c):
            update = lax.dot_general(
                projected, w[t, columns(c), :], (((1,), (1,)), ((), ())),
                preferred_element_type=jnp.float32,
            )
            x = buf[here, :, columns(c)].reshape(tall, chunk).astype(jnp.float32)
            buf[here, :, columns(c)] = (x + update).astype(jnp.bfloat16).reshape(many, block, chunk)
            after(c)

    def nothing(c):
        pass

    pair = q // 2

    @pl.when(pair == 0)
    def _():
        @pl.loop(q, 2)
        def _(t):
            apply(ha, t, 0, count, nothing, nothing)

    @pl.when(pair == 1)
    def _():
        @pl.loop(0, count)
        def _(m):
            @pl.loop(q, 4)
            def _(t):
                def after(c):
                    @pl.when(t == 3)
                    def _():
                        cross(m, c).start()

                apply(ha, t, m, 1, nothing, after)

    if owners > 2:
        hand_on(owners - 1, 0)
    hand_on(1, 1)
    if owners > 2:
        hand_on(owners - 1, 1)

    @pl.loop(0, 2 * owners)
    def _(j):
        far_to_near(j).wait_recv()

    @pl.when(q == 0)
    def _():
        @pl.loop(2, 4)
        def _(t):
            def after(c):
                @pl.when(t == 3)
                def _():
                    for m in range(count):
                        cross(m, c).start()

            apply(ha, t, 0, count, nothing, after)

    @pl.when(q == 1)
    def _():
        @pl.loop(0, count)
        def _(m):
            @pl.loop(2, 4)
            def _(t):
                def after(c):
                    @pl.when(t == 3)
                    def _():
                        cross(m, c).start()

                apply(ha, t, m, 1, nothing, after)

    @pl.loop(0, count)
    def _(m):
        @pl.loop(0, q)
        def _(t):
            def before(c):
                @pl.when(t == 0)
                def _():
                    cross(m, c).wait_recv()

            def after(c):
                @pl.when(t == q - 1)
                def _():
                    store(m, c).start()

            apply(hb, t, m, 1, before, after)

        @pl.when(q == 0)
        def _():
            @pl.loop(0, chunks)
            def _(c):
                cross(m, c).wait_recv()
                store(m, c).start()

    @pl.loop(0, count)
    def _(m):
        @pl.loop(0, chunks)
        def _(c):
            cross(m, c).wait_send()
            store(m, c).wait()

    for i in range(2 * owners):
        def drain(j, i=i):
            g = 2 * j + i % 2
            if i != 3:
                to_far(g).wait_send()
            to_near(g).wait_send()
            far_to_near(g).wait_send()

        at_distance(i // 2, drain)

    @pl.when(r > 0)
    def _():
        lower_left(2 * r + 1).wait_send()

    @pl.when(r < owners - 1)
    def _():
        lower_right(2 * r + 1).wait_send()


def per_device(sections, owners, master_weights, first_moment, second_moment, gradient_shard,
               hidden_states):
    new_master, new_first, new_second = adamw_update(
        master_weights, first_moment, second_moment, gradient_shard
    )
    local_rows = new_master[0].astype(jnp.bfloat16)
    hidden = hidden_states[0]
    count, block, width = hidden.shape
    columns = local_rows.shape[1]
    chunks = width // 1024
    moved = pl.pallas_call(
        functools.partial(relay, sections, owners),
        out_shape=jax.ShapeDtypeStruct(hidden.shape, hidden.dtype),
        in_specs=[pl.BlockSpec(memory_space=pl.ANY)] * 2,
        out_specs=pl.BlockSpec(memory_space=pl.ANY),
        scratch_shapes=[
            pltpu.VMEM((4, width, columns), jnp.bfloat16),
            pltpu.VMEM((count, block, width), jnp.bfloat16),
            pltpu.VMEM((count, block, width), jnp.bfloat16),
            pltpu.VMEM((count * block, columns), jnp.float32),
            pltpu.SemaphoreType.DMA((2,)),
            pltpu.SemaphoreType.DMA((4, 2 * owners)),
            pltpu.SemaphoreType.DMA((3, 2 * owners)),
            pltpu.SemaphoreType.DMA((5, 2 * owners)),
            pltpu.SemaphoreType.DMA((count, chunks)),
            pltpu.SemaphoreType.DMA((count, chunks)),
            pltpu.SemaphoreType.DMA((count, chunks)),
        ],
        compiler_params=pltpu.CompilerParams(
            collective_id=0, has_side_effects=True, vmem_limit_bytes=46 * 1024 * 1024
        ),
        cost_estimate=pl.CostEstimate(
            flops=ROUNDS * count * block * width * columns * 4,
            bytes_accessed=4 * count * block * width,
            transcendentals=0,
        ),
    )(local_rows, hidden)
    return (new_master, new_first, new_second, moved[None])


def solution(mesh):
    placed = (
        P("section", "dp", None),
        P("section", "dp", None),
        P("section", "dp", None),
        P("section", "dp", None),
        P("section", None, "dp", None),
    )
    return jax.shard_map(
        functools.partial(per_device, mesh.shape["section"], mesh.shape["dp"]),
        mesh=mesh,
        in_specs=placed,
        out_specs=(
            P("section", "dp", None),
            P("section", "dp", None),
            P("section", "dp", None),
            P("section", None, "dp", None),
        ),
        check_vma=False,
    )
```

```python
import functools

import jax
import jax.numpy as jnp
from jax import lax
from jax.experimental import pallas as pl
from jax.experimental.pallas import tpu as pltpu
from jax.sharding import PartitionSpec as P

ROUNDS = 4
ADAM_STEP = 1000
MESH = pl.DeviceIdType.MESH


beta_one = 0.9
beta_two = 0.95
learn_rate = 0.0003
decay_rate = 0.1
adam_eps = 1e-08
norm_eps = 1e-05


def adamw_update(master, moment, second, gradient):
    moment_new = beta_one * moment + (1.0 - beta_one) * gradient
    second_new = beta_two * second + (1.0 - beta_two) * gradient * gradient
    corr_one = 1.0 - beta_one**ADAM_STEP
    corr_two = 1.0 - beta_two**ADAM_STEP
    step_size = moment_new / corr_one / (jnp.sqrt(second_new / corr_two) + adam_eps)
    master_new = master - learn_rate * (step_size + decay_rate * master)
    return (master_new, moment_new, second_new)


def relay(sections, owners, shard_ref, hidden_ref, out_ref, w, ha, hb, acc,
          load_sem, zsend, psend, precv, ysend, yrecv, osem):
    s = lax.axis_index("section")
    r = lax.axis_index("dp")
    q = s % 4
    base = s - q
    near = q + 1 - 2 * (q % 2)
    far = (q + 2) % 4
    last = (near + 2) % 4
    near_dev = (base + near, r)
    far_dev = (base + far, r)
    ahead = ((s + 4) % sections, r)
    behind = ((s + sections - 4) % sections, r)
    rows = shard_ref.shape[0]
    width = hidden_ref.shape[2]
    count, block = hidden_ref.shape[0], hidden_ref.shape[1]
    chunks = ysend.shape[1]
    chunk = width // chunks

    half = rows // 2

    def piece(slot, g, send, recv, device):
        ref = w.at[slot, pl.ds(pl.multiple_of(g * half, half), half)]
        return pltpu.make_async_remote_copy(
            src_ref=ref, dst_ref=ref, send_sem=send, recv_sem=recv,
            device_id=device, device_id_type=MESH,
        )

    def right(g):
        return piece(q, g, zsend.at[0, g], precv.at[0, g], (s, r + 1))

    def left(g):
        return piece(q, g, zsend.at[1, g], precv.at[0, g], (s, r - 1))

    def to_far(g):
        return piece(q, g, psend.at[0, g], precv.at[1, g], far_dev)

    def to_near(g):
        return piece(q, g, psend.at[1, g], precv.at[2, g], near_dev)

    def far_to_near(g):
        return piece(far, g, psend.at[2, g], precv.at[3, g], near_dev)

    def lower_right(g):
        return piece(far, g, zsend.at[2, g], precv.at[4, g], (s, r + 1))

    def lower_left(g):
        return piece(far, g, zsend.at[3, g], precv.at[4, g], (s, r - 1))

    def at_distance(k, use):
        @pl.when(r - k >= 0)
        def _():
            use(r - k)

        if k:
            @pl.when(r + k < owners)
            def _():
                use(r + k)

    def columns(c):
        return pl.ds(pl.multiple_of(c * chunk, chunk), chunk)

    def cross(m, c):
        return pltpu.make_async_remote_copy(
            src_ref=ha.at[m, :, columns(c)], dst_ref=hb.at[m, :, columns(c)],
            send_sem=ysend.at[m, c], recv_sem=yrecv.at[m, c],
            device_id=ahead, device_id_type=MESH,
        )

    def store(m, c):
        return pltpu.make_async_copy(
            hb.at[m, :, columns(c)], out_ref.at[m, :, columns(c)], osem.at[m, c]
        )

    own = w.at[q, pl.ds(pl.multiple_of(r * rows, rows), rows)]
    load_w = pltpu.make_async_copy(shard_ref, own, load_sem.at[0])
    load_h = pltpu.make_async_copy(hidden_ref, ha, load_sem.at[1])
    load_w.start()
    load_h.start()

    barrier = pltpu.get_barrier_semaphore()
    partners = [near_dev, far_dev, ahead]
    if (2 * 4) % sections:
        partners.append(behind)
    for device in partners:
        pl.semaphore_signal(barrier, inc=1, device_id=device, device_id_type=MESH)

    @pl.when(r < owners - 1)
    def _():
        pl.semaphore_signal(barrier, inc=1, device_id=(s, r + 1), device_id_type=MESH)

    @pl.when(r > 0)
    def _():
        pl.semaphore_signal(barrier, inc=1, device_id=(s, r - 1), device_id_type=MESH)

    along = jnp.minimum(r, 1) + jnp.minimum(owners - 1 - r, 1)
    pl.semaphore_wait(barrier, len(partners) + along)

    load_w.wait()
    for i in range(2 * owners):
        k, h = divmod(i, 2)
        before_k, before_h = divmod(i - 1, 2)

        def arrive(j, i=i, h=h):
            g = 2 * j + h
            if i >= 2:
                left(g).wait_recv()
            if i != 3:
                to_far(g).start()
            to_near(g).start()

        at_distance(k, arrive)

        @pl.when((r > 0) & (r + k < owners))
        def _(i=i, k=k, h=h, before_k=before_k, before_h=before_h):
            if i:
                left(2 * (r + before_k) + before_h).wait_send()
            left(2 * (r + k) + h).start()

        @pl.when((r < owners - 1) & (r - k >= 0))
        def _(i=i, k=k, h=h, before_k=before_k, before_h=before_h):
            if i:
                right(2 * (r - before_k) + before_h).wait_send()
            right(2 * (r - k) + h).start()

        if i == 2:
            for g in (2 * r, 2 * r + 1):
                to_far(g).wait_recv()
                far_to_near(g).start()

        if i >= 2 and h == 0:
            @pl.when((r > 0) & (r + k == owners))
            def _():
                left(2 * owners - 1).wait_send()
                lower_left(2 * r + 1).start()

            @pl.when((r < owners - 1) & (r - k == -1))
            def _():
                right(1).wait_send()
                lower_right(2 * r + 1).start()

    def hand_on(k, h):
        def use(j):
            g = 2 * j + h
            if (k, h) == (1, 1):
                lower_left(g).wait_recv()
            else:
                to_far(g).wait_recv()
            far_to_near(g).start()

        at_distance(k, use)

    hand_on(1, 0)
    for k in range(2, owners - 1):
        hand_on(k, 0)
        hand_on(k, 1)

    @pl.loop(0, 2 * owners)
    def _(j):
        to_near(j).wait_recv()

    load_h.wait()

    def apply(buf, t, first, many, before, after):
        tall = many * block
        here = pl.ds(first, many)
        acc[:tall] = jnp.zeros((tall, acc.shape[1]), jnp.float32)

        def project(c, total):
            before(c)
            x = buf[here, :, columns(c)].reshape(tall, chunk)
            acc[:tall] += jnp.dot(x, w[t, columns(c), :], preferred_element_type=jnp.float32)
            flat = x.astype(jnp.float32)
            return total + jnp.sum(flat * flat, axis=-1, keepdims=True)

        total = lax.fori_loop(0, chunks, project, jnp.zeros((tall, 1), jnp.float32))
        scale = lax.rsqrt(total * (1.0 / width) + norm_eps)
        projected = (acc[:tall] * scale).astype(jnp.bfloat16)

        @pl.loop(0, chunks)
        def _(c):
            update = lax.dot_general(
                projected, w[t, columns(c), :], (((1,), (1,)), ((), ())),
                preferred_element_type=jnp.float32,
            )
            x = buf[here, :, columns(c)].reshape(tall, chunk).astype(jnp.float32)
            buf[here, :, columns(c)] = (x + update).astype(jnp.bfloat16).reshape(many, block, chunk)
            after(c)

    def nothing(c):
        pass

    pair = q // 2

    def hand_on_early():
        if owners > 2:
            hand_on(owners - 1, 0)

    def hand_on_late():
        hand_on(1, 1)
        if owners > 2:
            hand_on(owners - 1, 1)

    @pl.when(q == 0)
    def _():
        apply(ha, 0, 0, count, nothing, nothing)
        hand_on_early()
        apply(ha, 1, 0, 1, nothing, nothing)
        hand_on_late()

        @pl.loop(1, count)
        def _(m):
            apply(ha, 1, m, 1, nothing, nothing)

    @pl.when(q == 1)
    def _():
        apply(ha, 1, 0, count, nothing, nothing)
        hand_on_early()
        hand_on_late()

    @pl.when(pair == 1)
    def _():
        @pl.loop(0, count)
        def _(m):
            @pl.loop(q, 4)
            def _(t):
                def after(c):
                    @pl.when(t == 3)
                    def _():
                        cross(m, c).start()

                apply(ha, t, m, 1, nothing, after)

        hand_on_early()
        hand_on_late()

    @pl.loop(0, 2 * owners)
    def _(j):
        far_to_near(j).wait_recv()

    @pl.when(pair == 0)
    def _():
        @pl.loop(0, count)
        def _(m):
            @pl.loop(2, 4)
            def _(t):
                def after(c):
                    @pl.when(t == 3)
                    def _():
                        cross(m, c).start()

                apply(ha, t, m, 1, nothing, after)

    @pl.loop(0, count)
    def _(m):
        @pl.loop(0, q)
        def _(t):
            def before(c):
                @pl.when(t == 0)
                def _():
                    cross(m, c).wait_recv()

            def after(c):
                @pl.when(t == q - 1)
                def _():
                    store(m, c).start()

            apply(hb, t, m, 1, before, after)

        @pl.when(q == 0)
        def _():
            @pl.loop(0, chunks)
            def _(c):
                cross(m, c).wait_recv()
                store(m, c).start()

    @pl.loop(0, count)
    def _(m):
        @pl.loop(0, chunks)
        def _(c):
            cross(m, c).wait_send()
            store(m, c).wait()

    for i in range(2 * owners):
        def drain(j, i=i):
            g = 2 * j + i % 2
            if i != 3:
                to_far(g).wait_send()
            to_near(g).wait_send()
            far_to_near(g).wait_send()

        at_distance(i // 2, drain)

    @pl.when(r > 0)
    def _():
        lower_left(2 * r + 1).wait_send()

    @pl.when(r < owners - 1)
    def _():
        lower_right(2 * r + 1).wait_send()


def per_device(sections, owners, master_weights, first_moment, second_moment, gradient_shard,
               hidden_states):
    new_master, new_first, new_second = adamw_update(
        master_weights, first_moment, second_moment, gradient_shard
    )
    local_rows = new_master[0].astype(jnp.bfloat16)
    hidden = hidden_states[0]
    count, block, width = hidden.shape
    columns = local_rows.shape[1]
    chunks = width // 1024
    moved = pl.pallas_call(
        functools.partial(relay, sections, owners),
        out_shape=jax.ShapeDtypeStruct(hidden.shape, hidden.dtype),
        in_specs=[pl.BlockSpec(memory_space=pl.ANY)] * 2,
        out_specs=pl.BlockSpec(memory_space=pl.ANY),
        scratch_shapes=[
            pltpu.VMEM((4, width, columns), jnp.bfloat16),
            pltpu.VMEM((count, block, width), jnp.bfloat16),
            pltpu.VMEM((count, block, width), jnp.bfloat16),
            pltpu.VMEM((count * block, columns), jnp.float32),
            pltpu.SemaphoreType.DMA((2,)),
            pltpu.SemaphoreType.DMA((4, 2 * owners)),
            pltpu.SemaphoreType.DMA((3, 2 * owners)),
            pltpu.SemaphoreType.DMA((5, 2 * owners)),
            pltpu.SemaphoreType.DMA((count, chunks)),
            pltpu.SemaphoreType.DMA((count, chunks)),
            pltpu.SemaphoreType.DMA((count, chunks)),
        ],
        compiler_params=pltpu.CompilerParams(
            collective_id=0, has_side_effects=True, vmem_limit_bytes=46 * 1024 * 1024
        ),
        cost_estimate=pl.CostEstimate(
            flops=ROUNDS * count * block * width * columns * 4,
            bytes_accessed=4 * count * block * width,
            transcendentals=0,
        ),
    )(local_rows, hidden)
    return (new_master, new_first, new_second, moved[None])


def solution(mesh):
    placed = (
        P("section", "dp", None),
        P("section", "dp", None),
        P("section", "dp", None),
        P("section", "dp", None),
        P("section", None, "dp", None),
    )
    return jax.shard_map(
        functools.partial(per_device, mesh.shape["section"], mesh.shape["dp"]),
        mesh=mesh,
        in_specs=placed,
        out_specs=(
            P("section", "dp", None),
            P("section", "dp", None),
            P("section", "dp", None),
            P("section", None, "dp", None),
        ),
        check_vma=False,
    )
```

```python
import functools

import jax
import jax.numpy as jnp
from jax import lax
from jax.experimental import pallas as pl
from jax.experimental.pallas import tpu as pltpu
from jax.sharding import PartitionSpec as P

ROUNDS = 4
ADAM_STEP = 1000
MESH = pl.DeviceIdType.MESH


beta_one = 0.9
beta_two = 0.95
learn_rate = 0.0003
decay_rate = 0.1
adam_eps = 1e-08
norm_eps = 1e-05


def adamw_update(master, moment, second, gradient):
    moment_new = beta_one * moment + (1.0 - beta_one) * gradient
    second_new = beta_two * second + (1.0 - beta_two) * gradient * gradient
    corr_one = 1.0 - beta_one**ADAM_STEP
    corr_two = 1.0 - beta_two**ADAM_STEP
    step_size = moment_new / corr_one / (jnp.sqrt(second_new / corr_two) + adam_eps)
    master_new = master - learn_rate * (step_size + decay_rate * master)
    return (master_new, moment_new, second_new)


def relay(sections, owners, shard_ref, hidden_ref, out_ref, w, ha, hb, acc,
          load_sem, zsend, psend, precv, ysend, yrecv, osem):
    s = lax.axis_index("section")
    r = lax.axis_index("dp")
    q = s % 4
    base = s - q
    near = q + 1 - 2 * (q % 2)
    far = (q + 2) % 4
    last = (near + 2) % 4
    near_dev = (base + near, r)
    far_dev = (base + far, r)
    ahead = ((s + 4) % sections, r)
    behind = ((s + sections - 4) % sections, r)
    rows = shard_ref.shape[0]
    width = hidden_ref.shape[2]
    count, block = hidden_ref.shape[0], hidden_ref.shape[1]
    chunks = ysend.shape[1]
    chunk = width // chunks

    half = rows // 2

    def piece(slot, g, send, recv, device):
        ref = w.at[slot, pl.ds(pl.multiple_of(g * half, half), half)]
        return pltpu.make_async_remote_copy(
            src_ref=ref, dst_ref=ref, send_sem=send, recv_sem=recv,
            device_id=device, device_id_type=MESH,
        )

    def right(g):
        return piece(q, g, zsend.at[0, g], precv.at[0, g], (s, r + 1))

    def left(g):
        return piece(q, g, zsend.at[1, g], precv.at[0, g], (s, r - 1))

    def to_far(g):
        return piece(q, g, psend.at[0, g], precv.at[1, g], far_dev)

    def to_near(g):
        return piece(q, g, psend.at[1, g], precv.at[2, g], near_dev)

    def far_to_near(g):
        return piece(far, g, psend.at[2, g], precv.at[3, g], near_dev)

    def lower_right(g):
        return piece(far, g, zsend.at[2, g], precv.at[4, g], (s, r + 1))

    def lower_left(g):
        return piece(far, g, zsend.at[3, g], precv.at[4, g], (s, r - 1))

    def at_distance(k, use):
        @pl.when(r - k >= 0)
        def _():
            use(r - k)

        if k:
            @pl.when(r + k < owners)
            def _():
                use(r + k)

    def columns(c):
        return pl.ds(pl.multiple_of(c * chunk, chunk), chunk)

    def cross(m, c):
        return pltpu.make_async_remote_copy(
            src_ref=ha.at[m, :, columns(c)], dst_ref=hb.at[m, :, columns(c)],
            send_sem=ysend.at[m, c], recv_sem=yrecv.at[m, c],
            device_id=ahead, device_id_type=MESH,
        )

    def store(m, c):
        return pltpu.make_async_copy(
            hb.at[m, :, columns(c)], out_ref.at[m, :, columns(c)], osem.at[m, c]
        )

    own = w.at[q, pl.ds(pl.multiple_of(r * rows, rows), rows)]
    load_w = pltpu.make_async_copy(shard_ref, own, load_sem.at[0])
    load_h = pltpu.make_async_copy(hidden_ref, ha, load_sem.at[1])
    load_w.start()
    load_h.start()

    barrier = pltpu.get_barrier_semaphore()
    partners = [near_dev, far_dev, ahead]
    if (2 * 4) % sections:
        partners.append(behind)
    for device in partners:
        pl.semaphore_signal(barrier, inc=1, device_id=device, device_id_type=MESH)

    @pl.when(r < owners - 1)
    def _():
        pl.semaphore_signal(barrier, inc=1, device_id=(s, r + 1), device_id_type=MESH)

    @pl.when(r > 0)
    def _():
        pl.semaphore_signal(barrier, inc=1, device_id=(s, r - 1), device_id_type=MESH)

    along = jnp.minimum(r, 1) + jnp.minimum(owners - 1 - r, 1)
    pl.semaphore_wait(barrier, len(partners) + along)

    load_w.wait()
    for i in range(2 * owners):
        k, h = divmod(i, 2)
        before_k, before_h = divmod(i - 1, 2)

        def arrive(j, i=i, h=h):
            g = 2 * j + h
            if i >= 2:
                left(g).wait_recv()
            if i != 3:
                to_far(g).start()
            to_near(g).start()

        at_distance(k, arrive)

        @pl.when((r > 0) & (r + k < owners))
        def _(i=i, k=k, h=h, before_k=before_k, before_h=before_h):
            if i:
                left(2 * (r + before_k) + before_h).wait_send()
            left(2 * (r + k) + h).start()

        @pl.when((r < owners - 1) & (r - k >= 0))
        def _(i=i, k=k, h=h, before_k=before_k, before_h=before_h):
            if i:
                right(2 * (r - before_k) + before_h).wait_send()
            right(2 * (r - k) + h).start()

        if i == 2:
            for g in (2 * r, 2 * r + 1):
                to_far(g).wait_recv()
                far_to_near(g).start()

        if i >= 2 and h == 0:
            @pl.when((r > 0) & (r + k == owners))
            def _():
                left(2 * owners - 1).wait_send()
                lower_left(2 * r + 1).start()

            @pl.when((r < owners - 1) & (r - k == -1))
            def _():
                right(1).wait_send()
                lower_right(2 * r + 1).start()

    def hand_on(k, h):
        def use(j):
            g = 2 * j + h
            if (k, h) == (1, 1):
                lower_left(g).wait_recv()
            else:
                to_far(g).wait_recv()
            far_to_near(g).start()

        at_distance(k, use)

    hand_on(1, 0)
    for k in range(2, owners - 1):
        hand_on(k, 0)
        hand_on(k, 1)

    @pl.loop(0, 2 * owners)
    def _(j):
        to_near(j).wait_recv()

    load_h.wait()

    def apply(buf, t, first, many, before, after):
        tall = many * block
        here = pl.ds(first, many)
        acc[:tall] = jnp.zeros((tall, acc.shape[1]), jnp.float32)

        def project(c, total):
            before(c)
            x = buf[here, :, columns(c)].reshape(tall, chunk)
            acc[:tall] += jnp.dot(x, w[t, columns(c), :], preferred_element_type=jnp.float32)
            flat = x.astype(jnp.float32)
            return total + jnp.sum(flat * flat, axis=-1, keepdims=True)

        total = lax.fori_loop(0, chunks, project, jnp.zeros((tall, 1), jnp.float32))
        scale = lax.rsqrt(total * (1.0 / width) + norm_eps)
        projected = (acc[:tall] * scale).astype(jnp.bfloat16)

        @pl.loop(0, chunks)
        def _(c):
            update = lax.dot_general(
                projected, w[t, columns(c), :], (((1,), (1,)), ((), ())),
                preferred_element_type=jnp.float32,
            )
            x = buf[here, :, columns(c)].reshape(tall, chunk).astype(jnp.float32)
            buf[here, :, columns(c)] = (x + update).astype(jnp.bfloat16).reshape(many, block, chunk)
            after(c)

    def nothing(c):
        pass

    pair = q // 2

    def hand_on_early():
        if owners > 2:
            hand_on(owners - 1, 0)

    def hand_on_late():
        hand_on(1, 1)
        if owners > 2:
            hand_on(owners - 1, 1)

    @pl.when(q == 0)
    def _():
        apply(ha, 0, 0, count, nothing, nothing)
        hand_on_early()
        apply(ha, 1, 0, 1, nothing, nothing)
        hand_on_late()

        @pl.loop(1, count)
        def _(m):
            apply(ha, 1, m, 1, nothing, nothing)

    @pl.when(q == 1)
    def _():
        apply(ha, 1, 0, count, nothing, nothing)
        hand_on_early()
        hand_on_late()

    @pl.when(pair == 1)
    def _():
        @pl.loop(0, count)
        def _(m):
            @pl.loop(q, 4)
            def _(t):
                def after(c):
                    @pl.when(t == 3)
                    def _():
                        cross(m, c).start()

                apply(ha, t, m, 1, nothing, after)

        hand_on_early()
        hand_on_late()

    @pl.loop(0, 2 * owners)
    def _(j):
        far_to_near(j).wait_recv()

    @pl.when(pair == 0)
    def _():
        @pl.loop(0, count)
        def _(m):
            @pl.loop(2, 4)
            def _(t):
                def after(c):
                    @pl.when(t == 3)
                    def _():
                        cross(m, c).start()

                apply(ha, t, m, 1, nothing, after)

    @pl.loop(0, count)
    def _(m):
        @pl.loop(0, q)
        def _(t):
            def before(c):
                @pl.when(t == 0)
                def _():
                    cross(m, c).wait_recv()

            def after(c):
                @pl.when(t == q - 1)
                def _():
                    store(m, c).start()

            apply(hb, t, m, 1, before, after)

        @pl.when(q == 0)
        def _():
            @pl.loop(0, chunks)
            def _(c):
                cross(m, c).wait_recv()
                store(m, c).start()

    @pl.loop(0, count)
    def _(m):
        @pl.loop(0, chunks)
        def _(c):
            cross(m, c).wait_send()
            store(m, c).wait()

    for i in range(2 * owners):
        def drain(j, i=i):
            g = 2 * j + i % 2
            if i != 3:
                to_far(g).wait_send()
            to_near(g).wait_send()
            far_to_near(g).wait_send()

        at_distance(i // 2, drain)

    @pl.when(r > 0)
    def _():
        lower_left(2 * r + 1).wait_send()

    @pl.when(r < owners - 1)
    def _():
        lower_right(2 * r + 1).wait_send()


def per_device(sections, owners, master_weights, first_moment, second_moment, gradient_shard,
               hidden_states):
    new_master, new_first, new_second = adamw_update(
        master_weights, first_moment, second_moment, gradient_shard
    )
    local_rows = new_master[0].astype(jnp.bfloat16)
    hidden = hidden_states[0]
    count, block, width = hidden.shape
    columns = local_rows.shape[1]
    chunks = width // 2048
    moved = pl.pallas_call(
        functools.partial(relay, sections, owners),
        out_shape=jax.ShapeDtypeStruct(hidden.shape, hidden.dtype),
        in_specs=[pl.BlockSpec(memory_space=pl.ANY)] * 2,
        out_specs=pl.BlockSpec(memory_space=pl.ANY),
        scratch_shapes=[
            pltpu.VMEM((4, width, columns), jnp.bfloat16),
            pltpu.VMEM((count, block, width), jnp.bfloat16),
            pltpu.VMEM((count, block, width), jnp.bfloat16),
            pltpu.VMEM((count * block, columns), jnp.float32),
            pltpu.SemaphoreType.DMA((2,)),
            pltpu.SemaphoreType.DMA((4, 2 * owners)),
            pltpu.SemaphoreType.DMA((3, 2 * owners)),
            pltpu.SemaphoreType.DMA((5, 2 * owners)),
            pltpu.SemaphoreType.DMA((count, chunks)),
            pltpu.SemaphoreType.DMA((count, chunks)),
            pltpu.SemaphoreType.DMA((count, chunks)),
        ],
        compiler_params=pltpu.CompilerParams(
            collective_id=0, has_side_effects=True, vmem_limit_bytes=46 * 1024 * 1024
        ),
        cost_estimate=pl.CostEstimate(
            flops=ROUNDS * count * block * width * columns * 4,
            bytes_accessed=4 * count * block * width,
            transcendentals=0,
        ),
    )(local_rows, hidden)
    return (new_master, new_first, new_second, moved[None])


def solution(mesh):
    placed = (
        P("section", "dp", None),
        P("section", "dp", None),
        P("section", "dp", None),
        P("section", "dp", None),
        P("section", None, "dp", None),
    )
    return jax.shard_map(
        functools.partial(per_device, mesh.shape["section"], mesh.shape["dp"]),
        mesh=mesh,
        in_specs=placed,
        out_specs=(
            P("section", "dp", None),
            P("section", "dp", None),
            P("section", "dp", None),
            P("section", None, "dp", None),
        ),
        check_vma=False,
    )
```
